256 devices in a mesh: row: 16 (over y_lo, z), tp: 16 (over x, y_hi, core).
Axes of the slice: x: 4, y: 4 (y_hi: 2, y_lo: 2; y = y_hi * 2 + y_lo), z: 8, core: 2. Of those that a mesh axis runs over, the one named last changes fastest.
Arguments:
- feature_map: bfloat16 [1, 128, 128, 4096], P(None, 'row', None, 'tp'), may hold values from -6 to 6
- conv_weight: bfloat16 [3, 64, 64, 576], P(None, 'tp'), may hold values from -0.25 to 0.25
- branch_bias: float32 [3, 4096], P(None, 'tp'), may hold values from -3 to 3
- unite_weight: bfloat16 [3, 4096, 1024], P(None, 'tp'), may hold values from -0.0546875 to 0.0546875
Outputs:
- head_out: bfloat16 [1, 128, 128, 1024], P(None, 'row', 'tp')
The draws below stay inside these ranges and needn't reach their ends.
All inputs are finite; a program needn't handle non-finite values.
Results may differ from the reference program's by a relative error of at most 0.0049.
Values may be sent and summed in bfloat16 or wider, within the bound.
No kernel may reach another device: no remote copies, remote signals or barrier semaphores. Data moves between devices by JAX's collectives and lax.ppermute only.
A program may use at most 64 MiB of HBM per device.

```python
import jax
import jax.numpy as jnp
from jax import lax

C = 4096
GROUP = 64
UNITE = 1024
W = 128
TILES = 1
H = 128
GROUPS = 64
FIRST_SPACING = 8
SECOND_SPACING = 16
THIRD_SPACING = 32


def steps_of(stream_key, extent, cuts, least, largest):
    gain, own = 1.0, jax.random.fold_in(stream_key, 6)
    for axis_at, parts in cuts:
        steps = jnp.exp(jax.random.uniform(jax.random.fold_in(own, axis_at), (parts,), jnp.float32, least / len(cuts), largest / len(cuts)))
        gain = gain * jnp.repeat(steps, extent[axis_at] // parts).reshape([-1 if axis == axis_at else 1 for axis in range(len(extent))])
    return gain


def centred(stream_key, dims, width, reach, split=(), dtype=jnp.bfloat16):
    entries = width * jax.random.normal(stream_key, dims, jnp.float32)
    if split:
        entries = entries * steps_of(stream_key, dims, split, -0.22, 0.18)
    return jnp.clip(entries, -reach, reach).astype(dtype)


def setup_inputs(seed: int = 0) -> dict:
    splits = jax.random.split(jax.random.key(seed), 5)
    return {
        "feature_map": centred(splits[0], (TILES, H, W, C), 1.0, 6.0, ((1, 16), (3, 16))),
        "conv_weight": centred(splits[1], (3, GROUPS, GROUP, 9 * GROUP), (9 * GROUP) ** -0.5, 0.25, ((1, 16),)),
        "branch_bias": centred(splits[2], (3, C), 0.5, 3.0, ((1, 16),), jnp.float32),
        "unite_weight": centred(splits[3], (3, C, UNITE), (3 * C) ** -0.5, 0.0546875, ((1, 16),)),
    }


def reference(feature_map, conv_weight, branch_bias, unite_weight):
    def one_tile(tile_map):
        source_map = tile_map.astype(jnp.float32)[None]
        total = jnp.zeros((H, W, UNITE), jnp.float32)
        for arm_index, kernel_spacing in enumerate((FIRST_SPACING, SECOND_SPACING, THIRD_SPACING)):
            kernel = conv_weight[arm_index].astype(jnp.float32).reshape(GROUPS, GROUP, 3, 3, GROUP)
            kernel = kernel.transpose(2, 3, 4, 0, 1).reshape(3, 3, GROUP, C)
            summed = lax.conv_general_dilated(
                source_map, kernel, (1, 1), ((kernel_spacing, kernel_spacing), (kernel_spacing, kernel_spacing)),
                rhs_dilation=(kernel_spacing, kernel_spacing), dimension_numbers=("NHWC", "HWIO", "NHWC"),
                feature_group_count=GROUPS, precision=lax.Precision.HIGHEST)[0]
            hidden = jax.nn.gelu(summed + branch_bias[arm_index], approximate=False).astype(jnp.bfloat16)
            total = total + jnp.dot(hidden, unite_weight[arm_index], preferred_element_type=jnp.float32)
        return total.astype(jnp.bfloat16)

    return lax.map(one_tile, feature_map)
```

```python
import jax
import jax.numpy as jnp
from jax import lax
from jax.experimental import pallas as pl
from jax.experimental.pallas import tpu as pltpu
from jax.sharding import PartitionSpec as P


DISTANCES = (1, 2, 4)
BANDS = 16
SPOTS = 16
LOW = 4
PIXELS = BANDS * LOW
PAD = 4
TAPS = 9


def swap_halves(even, odd):
    low = lax.broadcasted_iota(jnp.int32, even.shape, even.ndim - 2) < LOW
    axis = even.ndim - 2
    first = jnp.where(low, even, pltpu.roll(odd, LOW, axis))
    second = jnp.where(low, pltpu.roll(even, LOW, axis), odd)
    return first, second


def pack_kernel(x_ref, out_ref):
    chan = x_ref.shape[2]
    for j in range(8):
        v = x_ref[j].astype(jnp.float32).reshape(8, 2, 8, chan)
        first, second = swap_halves(v[:, 0], v[:, 1])
        out_ref[j] = first.reshape(PIXELS, chan).astype(jnp.bfloat16)
        out_ref[8 + j] = second.reshape(PIXELS, chan).astype(jnp.bfloat16)


def pack(x):
    return pl.pallas_call(
        pack_kernel,
        out_shape=jax.ShapeDtypeStruct((16, PIXELS, x.shape[2]), jnp.bfloat16),
        name="pack",
    )(x)


def widen_kernel(w_ref, out_ref):
    chan = w_ref.shape[1]
    rows = lax.broadcasted_iota(jnp.int32, (chan, chan), 0) // 64
    cols = lax.broadcasted_iota(jnp.int32, (chan, chan), 1) // 64
    same = rows == cols
    for tap in range(TAPS):
        start, width = (tap // 2) * 128, 128 if tap < 8 else 64
        shift = (tap % 2) * 64
        place = lax.broadcasted_iota(jnp.int32, (chan, width), 0) % 64 + shift
        pick = (place == lax.broadcasted_iota(jnp.int32, (chan, width), 1)).astype(jnp.float32).astype(jnp.bfloat16)
        for arm in range(3):
            slab = w_ref[arm, :, start : start + width]
            wide = lax.dot_general(pick, slab, (((1,), (1,)), ((), ())), preferred_element_type=jnp.float32)
            out_ref[arm, tap * chan : (tap + 1) * chan, :] = jnp.where(same, wide, 0.0).astype(jnp.bfloat16)


def widen(conv_weight):
    chan = conv_weight.shape[1] * conv_weight.shape[2]
    return pl.pallas_call(
        widen_kernel,
        out_shape=jax.ShapeDtypeStruct((3, TAPS * chan, chan), jnp.bfloat16),
        name="widen",
    )(conv_weight.reshape(3, chan, -1))


def shifted(v, by):
    chan = v.shape[1]
    row = lax.broadcasted_iota(jnp.int32, v.shape, 0)
    if by == 0:
        return v
    if by == LOW:
        return jnp.where(row >= LOW, pltpu.roll(v, LOW, 0), 0.0)
    if by == -LOW:
        return jnp.where(row < PIXELS - LOW, pltpu.roll(v, PIXELS - LOW, 0), 0.0)
    zeros = jnp.zeros((abs(by), chan), v.dtype)
    if by > 0:
        return jnp.concatenate([zeros, v[: PIXELS - by]], axis=0)
    return jnp.concatenate([v[-by:], zeros], axis=0)


SHIFTS = (0, 1, -1, 2, -2, 4, -4)


def head_kernel(core_ref, x_ref, w_ref, bias_ref, unite_ref, send_ref, keep_ref, s_ref):
    step = pl.program_id(0)
    chan = x_ref.shape[2]

    @pl.when(step == 0)
    def _():
        zeros = jnp.zeros((len(SHIFTS), PAD, PIXELS, chan), jnp.bfloat16)
        s_ref[:, :PAD] = zeros
        s_ref[:, PAD + SPOTS :] = zeros
        for quad in range(4):
            v = x_ref[:, quad * 16 : (quad + 1) * 16, :].astype(jnp.float32).reshape(8, 2, 2, 8, chan)
            halves = swap_halves(v[:, 0], v[:, 1])
            for pair in range(2):
                for side in range(2):
                    spot = PAD + 4 * quad + 2 * pair + side
                    mine = halves[side][:, pair].reshape(PIXELS, chan)
                    for at, shift in enumerate(SHIFTS):
                        s_ref[at, spot] = shifted(mine, LOW * shift).astype(jnp.bfloat16)

    core = core_ref[0]
    spots = [PAD + 4 * step + 2 * half + (side + core) % 2 for side in (1, 0) for half in (0, 1)]
    hidden = []
    for arm, distance in enumerate(DISTANCES):
        total = None
        for kh in range(3):
            at = SHIFTS.index((1 - kh) * distance)
            for kw in range(3):
                left = jnp.concatenate([s_ref[at, spot + (kw - 1) * distance] for spot in spots], axis=0)
                tap = 3 * kh + kw
                part = jnp.dot(left, w_ref[arm, tap * chan : (tap + 1) * chan, :], preferred_element_type=jnp.float32)
                total = part if total is None else total + part
        summed = total + bias_ref[arm : arm + 1, :]
        hidden.append((0.5 * summed * (1.0 + lax.erf(summed * (0.5**0.5)))).astype(jnp.bfloat16))
    term = None
    for arm in range(3):
        part = jnp.dot(hidden[arm], unite_ref[arm], preferred_element_type=jnp.float32)
        term = part if term is None else term + part
    term = term.astype(jnp.bfloat16).reshape(4, PIXELS, -1)
    send_ref[...] = term[:2]
    keep_ref[...] = term[2:]


def head_terms(core, x, wide, bias, unite):
    chan, width = x.shape[2], unite.shape[2]
    whole = lambda *dims: pl.BlockSpec(dims, lambda step, core: (0,) * len(dims))
    out = jax.ShapeDtypeStruct((8, PIXELS, width), jnp.bfloat16)
    out_spec = pl.BlockSpec((2, PIXELS, width), lambda step, core: (step, 0, 0))
    return pl.pallas_call(
        head_kernel,
        grid_spec=pltpu.PrefetchScalarGridSpec(
            num_scalar_prefetch=1,
            grid=(4,),
            in_specs=[whole(*x.shape), whole(*wide.shape), whole(*bias.shape), whole(*unite.shape)],
            out_specs=[out_spec, out_spec],
            scratch_shapes=[pltpu.VMEM((len(SHIFTS), SPOTS + 2 * PAD, PIXELS, chan), jnp.bfloat16)],
        ),
        out_shape=[out, out],
        compiler_params=pltpu.CompilerParams(vmem_limit_bytes=48 * 2**20),
        cost_estimate=pl.CostEstimate(flops=5 * 10**9, bytes_accessed=8 * 10**6, transcendentals=10**6),
        name="head",
    )(core, x, wide, bias, unite)


def on_device(feature_map, conv_weight, branch_bias, unite_weight):
    core = (lax.axis_index("tp") % 2).astype(jnp.int32).reshape(1)
    packed = pack(feature_map[0])
    wide = widen(conv_weight)
    mine = lax.all_to_all(packed, "row", 0, 0)
    send, keep = head_terms(core, mine, wide, branch_bias, unite_weight)
    other = lax.ppermute(send, "tp", [(i, i ^ 1) for i in range(16)])
    both = (keep.astype(jnp.float32) + other.astype(jnp.float32)).astype(jnp.bfloat16)
    chips = [[core_at + 2 * chip for chip in range(8)] for core_at in range(2)]
    terms = lax.all_to_all(both, "tp", 0, 0, axis_index_groups=chips)
    result = jnp.sum(terms.astype(jnp.float32), axis=0).astype(jnp.bfloat16)
    bands = lax.all_to_all(result.reshape(BANDS, LOW, -1), "row", 0, 0)
    width = bands.shape[2]
    return bands.reshape(2, 8, LOW, width).transpose(1, 0, 2, 3).reshape(1, 8, 8, width)


def solution(mesh):
    placed = (
        P(None, "row", None, "tp"),
        P(None, "tp", None, None),
        P(None, "tp"),
        P(None, "tp", None),
    )
    return jax.shard_map(
        on_device, mesh=mesh, in_specs=placed, out_specs=P(None, "row", "tp", None), check_vma=False
    )
```

```python
import functools

import jax
import jax.numpy as jnp
from jax import lax
from jax.experimental import pallas as pl
from jax.experimental.pallas import tpu as pltpu
from jax.sharding import PartitionSpec as P


DISTANCES = (1, 2, 4)
BANDS = 16
SPOTS = 16
LOW = 4
PIXELS = BANDS * LOW
PAD = 4
TAPS = 9
VMEM_SPEC = pl.BlockSpec(memory_space=pltpu.VMEM)


def in_vmem(array):
    return pltpu.with_memory_space_constraint(array, pltpu.VMEM)


def swap_halves(even, odd):
    low = lax.broadcasted_iota(jnp.int32, even.shape, even.ndim - 2) < LOW
    axis = even.ndim - 2
    first = jnp.where(low, even, pltpu.roll(odd, LOW, axis))
    second = jnp.where(low, pltpu.roll(even, LOW, axis), odd)
    return first, second


def pack_kernel(x_ref, out_ref):
    chan = x_ref.shape[2]
    for j in range(8):
        v = x_ref[j].astype(jnp.float32).reshape(8, 2, 8, chan)
        first, second = swap_halves(v[:, 0], v[:, 1])
        out_ref[j] = first.reshape(PIXELS, chan).astype(jnp.bfloat16)
        out_ref[8 + j] = second.reshape(PIXELS, chan).astype(jnp.bfloat16)


def pack(x):
    return pl.pallas_call(
        pack_kernel,
        out_specs=VMEM_SPEC,
        out_shape=pltpu.VMEM((16, PIXELS, x.shape[2]), jnp.bfloat16),
        compiler_params=pltpu.CompilerParams(vmem_limit_bytes=16 * 2**20),
        name="pack",
    )(x)


def widen_kernel(w_ref, out_ref):
    chan = w_ref.shape[1]
    rows = lax.broadcasted_iota(jnp.int32, (chan, chan), 0) // 64
    cols = lax.broadcasted_iota(jnp.int32, (chan, chan), 1) // 64
    same = rows == cols
    for tap in range(TAPS):
        start, width = (tap // 2) * 128, 128 if tap < 8 else 64
        shift = (tap % 2) * 64
        place = lax.broadcasted_iota(jnp.int32, (chan, width), 0) % 64 + shift
        pick = (place == lax.broadcasted_iota(jnp.int32, (chan, width), 1)).astype(jnp.float32).astype(jnp.bfloat16)
        for arm in range(3):
            slab = w_ref[arm, :, start : start + width]
            wide = lax.dot_general(pick, slab, (((1,), (1,)), ((), ())), preferred_element_type=jnp.float32)
            out_ref[arm, tap * chan : (tap + 1) * chan, :] = jnp.where(same, wide, 0.0).astype(jnp.bfloat16)


def widen(conv_weight):
    chan = conv_weight.shape[1] * conv_weight.shape[2]
    return pl.pallas_call(
        widen_kernel,
        out_shape=jax.ShapeDtypeStruct((3, TAPS * chan, chan), jnp.bfloat16),
        compiler_params=pltpu.CompilerParams(vmem_limit_bytes=16 * 2**20),
        name="widen",
    )(conv_weight.reshape(3, chan, -1))


def shifted(v, by):
    chan = v.shape[1]
    row = lax.broadcasted_iota(jnp.int32, v.shape, 0)
    if by == 0:
        return v
    if by == LOW:
        return jnp.where(row >= LOW, pltpu.roll(v, LOW, 0), 0.0)
    if by == -LOW:
        return jnp.where(row < PIXELS - LOW, pltpu.roll(v, PIXELS - LOW, 0), 0.0)
    zeros = jnp.zeros((abs(by), chan), v.dtype)
    if by > 0:
        return jnp.concatenate([zeros, v[: PIXELS - by]], axis=0)
    return jnp.concatenate([v[-by:], zeros], axis=0)


SHIFTS = (0, 1, -1, 2, -2, 4, -4)


def spread_kernel(x_ref, s_ref):
    chan = x_ref.shape[2]
    zeros = jnp.zeros((len(SHIFTS), PAD, PIXELS, chan), jnp.bfloat16)
    s_ref[:, :PAD] = zeros
    s_ref[:, PAD + SPOTS :] = zeros
    for quad in range(4):
        v = x_ref[:, quad * 16 : (quad + 1) * 16, :].astype(jnp.float32).reshape(8, 2, 2, 8, chan)
        halves = swap_halves(v[:, 0], v[:, 1])
        for pair in range(2):
            for side in range(2):
                spot = PAD + 4 * quad + 2 * pair + side
                mine = halves[side][:, pair].reshape(PIXELS, chan)
                for at, shift in enumerate(SHIFTS):
                    s_ref[at, spot] = shifted(mine, LOW * shift).astype(jnp.bfloat16)


def spread(x):
    return pl.pallas_call(
        spread_kernel,
        in_specs=[VMEM_SPEC],
        out_specs=VMEM_SPEC,
        out_shape=pltpu.VMEM((len(SHIFTS), SPOTS + 2 * PAD, PIXELS, x.shape[2]), jnp.bfloat16),
        compiler_params=pltpu.CompilerParams(vmem_limit_bytes=16 * 2**20),
        name="spread",
    )(x)


def added(*terms):
    return sum(term.astype(jnp.float32) for term in terms)


def far_kernel(keep_ref, other_ref, out_ref):
    for at in range(2):
        out_ref[at] = added(keep_ref[at], other_ref[at]).astype(jnp.bfloat16)


def mid_kernel(keep_ref, across_ref, out_ref):
    for at in range(2):
        out_ref[at] = added(keep_ref[at], across_ref[at])


def split_kernel(mid_ref, other_ref, first_ref, second_ref):
    for at, out_ref in enumerate((first_ref, second_ref)):
        out_ref[...] = added(mid_ref[at], other_ref[at]).astype(out_ref.dtype)


def near_kernel(keep_ref, other_ref, across_ref, first_ref, second_ref):
    for at, out_ref in enumerate((first_ref, second_ref)):
        out_ref[...] = added(keep_ref[at], other_ref[at], across_ref[at]).astype(out_ref.dtype)


def call_add(kernel, name, out, *terms):
    return pl.pallas_call(
        kernel,
        in_specs=[VMEM_SPEC] * len(terms),
        out_specs=[VMEM_SPEC] * len(out),
        out_shape=out,
        compiler_params=pltpu.CompilerParams(vmem_limit_bytes=8 * 2**20),
        name=name,
    )(*[in_vmem(term) for term in terms])


def head_kernel(chunk, spot_ref, s_ref, w_ref, bias_ref, unite_ref, *refs):
    send_ref, keep_ref = refs[-2:]
    chan = s_ref.shape[3]
    spots = [PAD + spot_ref[chunk, at] for at in range(4)]
    hidden = []
    for arm, distance in enumerate(DISTANCES):
        total = None
        for kh in range(3):
            at = SHIFTS.index((1 - kh) * distance)
            for kw in range(3):
                left = jnp.concatenate([s_ref[at, spot + (kw - 1) * distance] for spot in spots], axis=0)
                tap = 3 * kh + kw
                part = jnp.dot(left, w_ref[arm, tap * chan : (tap + 1) * chan, :], preferred_element_type=jnp.float32)
                total = part if total is None else total + part
        summed = total + bias_ref[arm : arm + 1, :]
        hidden.append((0.5 * summed * (1.0 + lax.erf(summed * (0.5**0.5)))).astype(jnp.bfloat16))
    term = None
    for arm in range(3):
        part = jnp.dot(hidden[arm], unite_ref[arm], preferred_element_type=jnp.float32)
        term = part if term is None else term + part
    term = term.reshape(4, PIXELS, -1)
    send_ref[...] = term[:2].astype(jnp.bfloat16)
    keep_ref[...] = term[2:]


def head_terms(chunk, spots, spread_x, wide, bias, unite, after):
    out = [pltpu.VMEM((2, PIXELS, unite.shape[2]), dtype) for dtype in (jnp.bfloat16, jnp.float32)]
    return pl.pallas_call(
        functools.partial(head_kernel, chunk),
        in_specs=[pl.BlockSpec(memory_space=pltpu.SMEM)] + [VMEM_SPEC] * 4 + [pl.BlockSpec(memory_space=pl.ANY)] * len(after),
        out_specs=[VMEM_SPEC] * 2,
        out_shape=out,
        compiler_params=pltpu.CompilerParams(vmem_limit_bytes=16 * 2**20),
        name="head",
    )(spots, spread_x, wide, bias, unite, *after)


CHUNKS = (((2, 1), (1, 1)), ((3, 1), (0, 1)), ((2, 0), (1, 0)), ((3, 0), (0, 0)))
SWAP = [(i, i ^ 1) for i in range(16)]
FAR = [(i, i ^ 2) for i in range(16)]


def hop(ahead):
    return [(i, (i + 4 * ahead) % 16) for i in range(16)]


def on_device(feature_map, conv_weight, branch_bias, unite_weight):
    at = lax.axis_index("tp").astype(jnp.int32)
    chip_x, chip_y, core = at // 4, (at // 2) % 2, at % 2
    spots = jnp.stack([
        jnp.stack([4 * ((chip_x + ahead) % 4) + 2 * ((chip_y + across) % 2) + (core + side) % 2 for side in (1, 0) for ahead, across in chunk])
        for chunk in CHUNKS
    ])
    packed = pack(feature_map[0])
    wide = in_vmem(widen(conv_weight))
    mine = lax.all_to_all(packed, "row", 0, 0)
    spread_x = spread(mine)
    unite, bias = in_vmem(unite_weight), in_vmem(branch_bias)
    width = unite_weight.shape[2]
    bf16, f32 = (pltpu.VMEM((PIXELS, width), dtype) for dtype in (jnp.bfloat16, jnp.float32))
    both = pltpu.VMEM((2, PIXELS, width), jnp.bfloat16)

    def head(chunk, *after):
        send, keep = head_terms(chunk, spots, spread_x, wide, bias, unite, after)
        return keep, lax.ppermute(send, "tp", SWAP)

    far0, far1 = head(0), head(1)
    (far0,) = call_add(far_kernel, "far", [both], *far0)
    across0 = lax.ppermute(far0, "tp", FAR)
    near0 = head(2, far0)
    (far1,) = call_add(far_kernel, "far", [both], *far1)
    across1 = lax.ppermute(far1, "tp", FAR)
    near1 = head(3, far1)
    opposite, following = call_add(near_kernel, "near", [bf16, bf16], *near0, across0)
    opposite, following = lax.ppermute(opposite, "tp", hop(2)), lax.ppermute(following, "tp", hop(1))
    keep1, other1 = near1
    (mid1,) = call_add(mid_kernel, "mid", [pltpu.VMEM((2, PIXELS, width), jnp.float32)], keep1, across1)
    previous, own = call_add(split_kernel, "split", [bf16, f32], mid1, other1)
    previous = lax.ppermute(previous, "tp", hop(3))
    result = added(own, opposite, following, previous).astype(jnp.bfloat16)
    bands = lax.all_to_all(result.reshape(BANDS, LOW, width), "row", 0, 0)
    return bands.reshape(2, 8, LOW, width).transpose(1, 0, 2, 3).reshape(1, 8, 8, width)


def solution(mesh):
    placed = (
        P(None, "row", None, "tp"),
        P(None, "tp", None, None),
        P(None, "tp"),
        P(None, "tp", None),
    )
    return jax.shard_map(
        on_device, mesh=mesh, in_specs=placed, out_specs=P(None, "row", "tp", None), check_vma=False
    )
```

```python
import functools

import jax
import jax.numpy as jnp
from jax import lax
from jax.experimental import pallas as pl
from jax.experimental.pallas import tpu as pltpu
from jax.sharding import PartitionSpec as P


DISTANCES = (1, 2, 4)
BANDS = 16
SPOTS = 16
LOW = 4
PIXELS = BANDS * LOW
PAD = 4
TAPS = 9
GROUP = 64
VMEM_SPEC = pl.BlockSpec(memory_space=pltpu.VMEM)


def in_vmem(array):
    return pltpu.with_memory_space_constraint(array, pltpu.VMEM)


def swap_halves(even, odd):
    low = lax.broadcasted_iota(jnp.int32, even.shape, even.ndim - 2) < LOW
    axis = even.ndim - 2
    first = jnp.where(low, even, pltpu.roll(odd, LOW, axis))
    second = jnp.where(low, pltpu.roll(even, LOW, axis), odd)
    return first, second


def pack_kernel(x_ref, out_ref):
    chan = x_ref.shape[2]
    for j in range(8):
        v = x_ref[j].astype(jnp.float32).reshape(8, 2, 8, chan)
        first, second = swap_halves(v[:, 0], v[:, 1])
        out_ref[j] = first.reshape(PIXELS, chan).astype(jnp.bfloat16)
        out_ref[8 + j] = second.reshape(PIXELS, chan).astype(jnp.bfloat16)


def pack(x):
    return pl.pallas_call(
        pack_kernel,
        out_specs=VMEM_SPEC,
        out_shape=pltpu.VMEM((16, PIXELS, x.shape[2]), jnp.bfloat16),
        compiler_params=pltpu.CompilerParams(vmem_limit_bytes=16 * 2**20),
        name="pack",
    )(x)


def turn_kernel(w_ref, out_ref):
    for tap in range(TAPS):
        start, width = (tap // 2) * 128, 128 if tap < 8 else 64
        place = lax.broadcasted_iota(jnp.int32, (GROUP, width), 0) + (tap % 2) * GROUP
        pick = (place == lax.broadcasted_iota(jnp.int32, (GROUP, width), 1)).astype(jnp.float32).astype(jnp.bfloat16)
        for arm in range(3):
            slab = w_ref[arm, :, start : start + width]
            turned = lax.dot_general(pick, slab, (((1,), (1,)), ((), ())), preferred_element_type=jnp.float32)
            out_ref[arm, tap * GROUP : (tap + 1) * GROUP, :] = turned.astype(jnp.bfloat16)


def turn(conv_weight):
    chan = conv_weight.shape[1] * conv_weight.shape[2]
    return pl.pallas_call(
        turn_kernel,
        in_specs=[VMEM_SPEC],
        out_specs=VMEM_SPEC,
        out_shape=pltpu.VMEM((3, TAPS * GROUP, chan), jnp.bfloat16),
        compiler_params=pltpu.CompilerParams(vmem_limit_bytes=16 * 2**20),
        name="turn",
    )(conv_weight.reshape(3, chan, -1))


def shifted(v, by):
    chan = v.shape[1]
    row = lax.broadcasted_iota(jnp.int32, v.shape, 0)
    if by == 0:
        return v
    if by == LOW:
        return jnp.where(row >= LOW, pltpu.roll(v, LOW, 0), 0.0)
    if by == -LOW:
        return jnp.where(row < PIXELS - LOW, pltpu.roll(v, PIXELS - LOW, 0), 0.0)
    zeros = jnp.zeros((abs(by), chan), v.dtype)
    if by > 0:
        return jnp.concatenate([zeros, v[: PIXELS - by]], axis=0)
    return jnp.concatenate([v[-by:], zeros], axis=0)


SHIFTS = (0, 1, -1, 2, -2, 4, -4)


def spread_kernel(x_ref, s_ref):
    chan = x_ref.shape[2]
    zeros = jnp.zeros((len(SHIFTS), PAD, PIXELS, chan), jnp.bfloat16)
    s_ref[:, :PAD] = zeros
    s_ref[:, PAD + SPOTS :] = zeros
    for quad in range(4):
        v = x_ref[:, quad * 16 : (quad + 1) * 16, :].astype(jnp.float32).reshape(8, 2, 2, 8, chan)
        halves = swap_halves(v[:, 0], v[:, 1])
        for pair in range(2):
            for side in range(2):
                spot = PAD + 4 * quad + 2 * pair + side
                mine = halves[side][:, pair].reshape(PIXELS, chan)
                for at, shift in enumerate(SHIFTS):
                    s_ref[at, spot] = shifted(mine, LOW * shift).astype(jnp.bfloat16)


def spread(x):
    return pl.pallas_call(
        spread_kernel,
        in_specs=[VMEM_SPEC],
        out_specs=VMEM_SPEC,
        out_shape=pltpu.VMEM((len(SHIFTS), SPOTS + 2 * PAD, PIXELS, x.shape[2]), jnp.bfloat16),
        compiler_params=pltpu.CompilerParams(vmem_limit_bytes=16 * 2**20),
        name="spread",
    )(x)


def added(*terms):
    return sum(term.astype(jnp.float32) for term in terms)


def far_kernel(keep_ref, other_ref, out_ref):
    for at in range(2):
        out_ref[at] = added(keep_ref[at], other_ref[at]).astype(jnp.bfloat16)


def mid_kernel(keep_ref, across_ref, out_ref):
    for at in range(2):
        out_ref[at] = added(keep_ref[at], across_ref[at])


def split_kernel(mid_ref, other_ref, first_ref, second_ref):
    for at, out_ref in enumerate((first_ref, second_ref)):
        out_ref[...] = added(mid_ref[at], other_ref[at]).astype(out_ref.dtype)


def near_kernel(keep_ref, other_ref, across_ref, first_ref, second_ref):
    for at, out_ref in enumerate((first_ref, second_ref)):
        out_ref[...] = added(keep_ref[at], other_ref[at], across_ref[at]).astype(out_ref.dtype)


def call_add(kernel, name, out, *terms):
    return pl.pallas_call(
        kernel,
        in_specs=[VMEM_SPEC] * len(terms),
        out_specs=[VMEM_SPEC] * len(out),
        out_shape=out,
        compiler_params=pltpu.CompilerParams(vmem_limit_bytes=8 * 2**20),
        name=name,
    )(*[in_vmem(term) for term in terms])


def head_kernel(chunk, spot_ref, s_ref, w_ref, bias_ref, unite_ref, *refs):
    send_ref, keep_ref = refs[-2:]
    chan = s_ref.shape[3]
    spots = [PAD + spot_ref[chunk, at] for at in range(4)]
    groups = chan // GROUP
    column = lax.broadcasted_iota(jnp.int32, (GROUP, chan), 1) // GROUP
    masks = [(column == group).astype(jnp.float32).astype(jnp.bfloat16) for group in range(groups)]
    hidden = []
    for arm, distance in enumerate(DISTANCES):
        total = None
        for kh in range(3):
            at = SHIFTS.index((1 - kh) * distance)
            for kw in range(3):
                left = jnp.concatenate([s_ref[at, spot + (kw - 1) * distance] for spot in spots], axis=0)
                tap = 3 * kh + kw
                narrow = w_ref[arm, tap * GROUP : (tap + 1) * GROUP, :]
                wide = jnp.concatenate([narrow * mask for mask in masks], axis=0)
                part = jnp.dot(left, wide, preferred_element_type=jnp.float32)
                total = part if total is None else total + part
        summed = total + bias_ref[arm : arm + 1, :]
        hidden.append((0.5 * summed * (1.0 + lax.erf(summed * (0.5**0.5)))).astype(jnp.bfloat16))
    term = None
    for arm in range(3):
        part = jnp.dot(hidden[arm], unite_ref[arm], preferred_element_type=jnp.float32)
        term = part if term is None else term + part
    term = term.reshape(4, PIXELS, -1)
    send_ref[...] = term[:2].astype(jnp.bfloat16)
    keep_ref[...] = term[2:]


def head_terms(chunk, spots, spread_x, wide, bias, unite, after):
    out = [pltpu.VMEM((2, PIXELS, unite.shape[2]), dtype) for dtype in (jnp.bfloat16, jnp.float32)]
    return pl.pallas_call(
        functools.partial(head_kernel, chunk),
        in_specs=[pl.BlockSpec(memory_space=pltpu.SMEM)] + [VMEM_SPEC] * 4 + [pl.BlockSpec(memory_space=pl.ANY)] * len(after),
        out_specs=[VMEM_SPEC] * 2,
        out_shape=out,
        compiler_params=pltpu.CompilerParams(vmem_limit_bytes=16 * 2**20),
        name="head",
    )(spots, spread_x, wide, bias, unite, *after)


CHUNKS = (((2, 1), (1, 1)), ((3, 1), (0, 1)), ((2, 0), (1, 0)), ((3, 0), (0, 0)))
SWAP = [(i, i ^ 1) for i in range(16)]
FAR = [(i, i ^ 2) for i in range(16)]


def hop(ahead):
    return [(i, (i + 4 * ahead) % 16) for i in range(16)]


def on_device(feature_map, conv_weight, branch_bias, unite_weight):
    at = lax.axis_index("tp").astype(jnp.int32)
    chip_x, chip_y, core = at // 4, (at // 2) % 2, at % 2
    spots = jnp.stack([
        jnp.stack([4 * ((chip_x + ahead) % 4) + 2 * ((chip_y + across) % 2) + (core + side) % 2 for side in (1, 0) for ahead, across in chunk])
        for chunk in CHUNKS
    ])
    packed = pack(feature_map[0])
    wide = in_vmem(turn(conv_weight))
    mine = lax.all_to_all(packed, "row", 0, 0)
    spread_x = spread(mine)
    unite, bias = in_vmem(unite_weight), in_vmem(branch_bias)
    width = unite_weight.shape[2]
    bf16, f32 = (pltpu.VMEM((PIXELS, width), dtype) for dtype in (jnp.bfloat16, jnp.float32))
    both = pltpu.VMEM((2, PIXELS, width), jnp.bfloat16)

    def head(chunk, *after):
        send, keep = head_terms(chunk, spots, spread_x, wide, bias, unite, after)
        return keep, lax.ppermute(send, "tp", SWAP)

    far0, far1 = head(0), head(1)
    (far0,) = call_add(far_kernel, "far", [both], *far0)
    across0 = lax.ppermute(far0, "tp", FAR)
    near0 = head(2, far0)
    (far1,) = call_add(far_kernel, "far", [both], *far1)
    across1 = lax.ppermute(far1, "tp", FAR)
    near1 = head(3, far1)
    opposite, following = call_add(near_kernel, "near", [bf16, bf16], *near0, across0)
    opposite, following = lax.ppermute(opposite, "tp", hop(2)), lax.ppermute(following, "tp", hop(1))
    keep1, other1 = near1
    (mid1,) = call_add(mid_kernel, "mid", [pltpu.VMEM((2, PIXELS, width), jnp.float32)], keep1, across1)
    previous, own = call_add(split_kernel, "split", [bf16, f32], mid1, other1)
    previous = lax.ppermute(previous, "tp", hop(3))
    result = added(own, opposite, following, previous).astype(jnp.bfloat16)
    bands = lax.all_to_all(result.reshape(BANDS, LOW, width), "row", 0, 0)
    return bands.reshape(2, 8, LOW, width).transpose(1, 0, 2, 3).reshape(1, 8, 8, width)


def solution(mesh):
    placed = (
        P(None, "row", None, "tp"),
        P(None, "tp", None, None),
        P(None, "tp"),
        P(None, "tp", None),
    )
    return jax.shard_map(
        on_device, mesh=mesh, in_specs=placed, out_specs=P(None, "row", "tp", None), check_vma=False
    )
```

```python
import functools

import jax
import jax.numpy as jnp
from jax import lax
from jax.experimental import pallas as pl
from jax.experimental.pallas import tpu as pltpu
from jax.sharding import PartitionSpec as P


DISTANCES = (1, 2, 4)
BANDS = 16
SPOTS = 16
LOW = 4
PIXELS = BANDS * LOW
PAD = 4
TAPS = 9
GROUP = 64
VMEM_SPEC = pl.BlockSpec(memory_space=pltpu.VMEM)


def in_vmem(array):
    return pltpu.with_memory_space_constraint(array, pltpu.VMEM)


def swap_halves(even, odd):
    low = lax.broadcasted_iota(jnp.int32, even.shape, even.ndim - 2) < LOW
    axis = even.ndim - 2
    first = jnp.where(low, even, pltpu.roll(odd, LOW, axis))
    second = jnp.where(low, pltpu.roll(even, LOW, axis), odd)
    return first, second


def pack_kernel(x_ref, out_ref):
    chan = x_ref.shape[2]
    for j in range(8):
        v = x_ref[j].astype(jnp.float32).reshape(8, 2, 8, chan)
        first, second = swap_halves(v[:, 0], v[:, 1])
        out_ref[j] = first.reshape(PIXELS, chan).astype(jnp.bfloat16)
        out_ref[8 + j] = second.reshape(PIXELS, chan).astype(jnp.bfloat16)


def pack(x):
    return pl.pallas_call(
        pack_kernel,
        out_specs=VMEM_SPEC,
        out_shape=pltpu.VMEM((16, PIXELS, x.shape[2]), jnp.bfloat16),
        compiler_params=pltpu.CompilerParams(vmem_limit_bytes=16 * 2**20),
        name="pack",
    )(x)


def turn_kernel(w_ref, out_ref):
    for tap in range(TAPS):
        start, width = (tap // 2) * 128, 128 if tap < 8 else 64
        place = lax.broadcasted_iota(jnp.int32, (GROUP, width), 0) + (tap % 2) * GROUP
        pick = (place == lax.broadcasted_iota(jnp.int32, (GROUP, width), 1)).astype(jnp.float32).astype(jnp.bfloat16)
        for arm in range(3):
            slab = w_ref[arm, :, start : start + width]
            turned = lax.dot_general(pick, slab, (((1,), (1,)), ((), ())), preferred_element_type=jnp.float32)
            out_ref[arm, tap * GROUP : (tap + 1) * GROUP, :] = turned.astype(jnp.bfloat16)


def turn(conv_weight):
    chan = conv_weight.shape[1] * conv_weight.shape[2]
    return pl.pallas_call(
        turn_kernel,
        in_specs=[VMEM_SPEC],
        out_specs=VMEM_SPEC,
        out_shape=pltpu.VMEM((3, TAPS * GROUP, chan), jnp.bfloat16),
        compiler_params=pltpu.CompilerParams(vmem_limit_bytes=16 * 2**20),
        name="turn",
    )(conv_weight.reshape(3, chan, -1))


def shifted(v, by):
    chan = v.shape[1]
    row = lax.broadcasted_iota(jnp.int32, v.shape, 0)
    if by == 0:
        return v
    if by == LOW:
        return jnp.where(row >= LOW, pltpu.roll(v, LOW, 0), 0.0)
    if by == -LOW:
        return jnp.where(row < PIXELS - LOW, pltpu.roll(v, PIXELS - LOW, 0), 0.0)
    zeros = jnp.zeros((abs(by), chan), v.dtype)
    if by > 0:
        return jnp.concatenate([zeros, v[: PIXELS - by]], axis=0)
    return jnp.concatenate([v[-by:], zeros], axis=0)


SHIFTS = (0, 1, -1, 2, -2, 4, -4)


def spread_kernel(x_ref, s_ref):
    chan = x_ref.shape[2]
    zeros = jnp.zeros((len(SHIFTS), PAD, PIXELS, chan), jnp.bfloat16)
    s_ref[:, :PAD] = zeros
    s_ref[:, PAD + SPOTS :] = zeros
    for quad in range(4):
        v = x_ref[:, quad * 16 : (quad + 1) * 16, :].astype(jnp.float32).reshape(8, 2, 2, 8, chan)
        halves = swap_halves(v[:, 0], v[:, 1])
        for pair in range(2):
            for side in range(2):
                spot = PAD + 4 * quad + 2 * pair + side
                mine = halves[side][:, pair].reshape(PIXELS, chan)
                for at, shift in enumerate(SHIFTS):
                    s_ref[at, spot] = shifted(mine, LOW * shift).astype(jnp.bfloat16)


def spread(x):
    return pl.pallas_call(
        spread_kernel,
        in_specs=[VMEM_SPEC],
        out_specs=VMEM_SPEC,
        out_shape=pltpu.VMEM((len(SHIFTS), SPOTS + 2 * PAD, PIXELS, x.shape[2]), jnp.bfloat16),
        compiler_params=pltpu.CompilerParams(vmem_limit_bytes=16 * 2**20),
        name="spread",
    )(x)


def added(*terms):
    return sum(term.astype(jnp.float32) for term in terms)


def far_kernel(keep_ref, other_ref, out_ref):
    for at in range(2):
        out_ref[at] = added(keep_ref[at], other_ref[at]).astype(jnp.bfloat16)


def mid_kernel(keep_ref, across_ref, out_ref):
    for at in range(2):
        out_ref[at] = added(keep_ref[at], across_ref[at])


def split_kernel(mid_ref, other_ref, first_ref, second_ref):
    for at, out_ref in enumerate((first_ref, second_ref)):
        out_ref[...] = added(mid_ref[at], other_ref[at]).astype(out_ref.dtype)


def near_kernel(keep_ref, other_ref, across_ref, first_ref, second_ref):
    for at, out_ref in enumerate((first_ref, second_ref)):
        out_ref[...] = added(keep_ref[at], other_ref[at], across_ref[at]).astype(out_ref.dtype)


def call_add(kernel, name, out, *terms):
    return pl.pallas_call(
        kernel,
        in_specs=[VMEM_SPEC] * len(terms),
        out_specs=[VMEM_SPEC] * len(out),
        out_shape=out,
        compiler_params=pltpu.CompilerParams(vmem_limit_bytes=8 * 2**20),
        name=name,
    )(*[in_vmem(term) for term in terms])


def head_kernel(chunk, spot_ref, s_ref, w_ref, bias_ref, unite_ref, *refs):
    send_ref, keep_ref = refs[-2:]
    chan = s_ref.shape[3]
    spots = [PAD + spot_ref[chunk, at] for at in range(4)]
    groups = chan // GROUP
    column = lax.broadcasted_iota(jnp.int32, (GROUP, chan), 1) // GROUP
    masks = [(column == group).astype(jnp.float32).astype(jnp.bfloat16) for group in range(groups)]
    hidden = []
    for arm, distance in enumerate(DISTANCES):
        total = None
        for kh in range(3):
            at = SHIFTS.index((1 - kh) * distance)
            for kw in range(3):
                left = jnp.concatenate([s_ref[at, spot + (kw - 1) * distance] for spot in spots], axis=0)
                tap = 3 * kh + kw
                narrow = w_ref[arm, tap * GROUP : (tap + 1) * GROUP, :]
                wide = jnp.concatenate([narrow * mask for mask in masks], axis=0)
                part = jnp.dot(left, wide, preferred_element_type=jnp.float32)
                total = part if total is None else total + part
        summed = total + bias_ref[arm : arm + 1, :]
        hidden.append((0.5 * summed * (1.0 + lax.erf(summed * (0.5**0.5)))).astype(jnp.bfloat16))
    term = None
    for arm in range(3):
        part = jnp.dot(hidden[arm], unite_ref[arm], preferred_element_type=jnp.float32)
        term = part if term is None else term + part
    term = term.reshape(4, PIXELS, -1)
    send_ref[...] = term[:2].astype(jnp.bfloat16)
    keep_ref[...] = term[2:]


def head_terms(chunk, spots, spread_x, wide, bias, unite, after):
    out = [pltpu.VMEM((2, PIXELS, unite.shape[2]), dtype) for dtype in (jnp.bfloat16, jnp.float32)]
    return pl.pallas_call(
        functools.partial(head_kernel, chunk),
        in_specs=[pl.BlockSpec(memory_space=pltpu.SMEM)] + [VMEM_SPEC] * 4 + [pl.BlockSpec(memory_space=pl.ANY)] * len(after),
        out_specs=[VMEM_SPEC] * 2,
        out_shape=out,
        compiler_params=pltpu.CompilerParams(vmem_limit_bytes=16 * 2**20),
        name="head",
    )(spots, spread_x, wide, bias, unite, *after)


CHUNKS = (((2, 1), (3, 1)), ((1, 1), (0, 1)), ((2, 0), (3, 0)), ((1, 0), (0, 0)))
SWAP = [(i, i ^ 1) for i in range(16)]
FAR = [(i, i ^ 2) for i in range(16)]


def hop(ahead):
    return [(i, (i + 4 * ahead) % 16) for i in range(16)]


def on_device(feature_map, conv_weight, branch_bias, unite_weight):
    at = lax.axis_index("tp").astype(jnp.int32)
    chip_x, chip_y, core = at // 4, (at // 2) % 2, at % 2
    spots = jnp.stack([
        jnp.stack([4 * ((chip_x + ahead) % 4) + 2 * ((chip_y + across) % 2) + (core + side) % 2 for side in (1, 0) for ahead, across in chunk])
        for chunk in CHUNKS
    ])
    packed = pack(feature_map[0])
    wide = in_vmem(turn(conv_weight))
    mine = lax.all_to_all(packed, "row", 0, 0)
    spread_x = spread(mine)
    unite, bias = in_vmem(unite_weight), in_vmem(branch_bias)
    width = unite_weight.shape[2]
    bf16, f32 = (pltpu.VMEM((PIXELS, width), dtype) for dtype in (jnp.bfloat16, jnp.float32))
    both = pltpu.VMEM((2, PIXELS, width), jnp.bfloat16)

    def head(chunk, *after):
        send, keep = head_terms(chunk, spots, spread_x, wide, bias, unite, after)
        return keep, lax.ppermute(send, "tp", SWAP)

    far0, far1 = head(0), head(1)
    (far0,) = call_add(far_kernel, "far", [both], *far0)
    across0 = lax.ppermute(far0, "tp", FAR)
    near0 = head(2, far0)
    (far1,) = call_add(far_kernel, "far", [both], *far1)
    across1 = lax.ppermute(far1, "tp", FAR)
    near1 = head(3, far1)
    opposite, following = call_add(near_kernel, "near", [bf16, bf16], *near0, across0)
    opposite, following = lax.ppermute(opposite, "tp", hop(2)), lax.ppermute(following, "tp", hop(3))
    keep1, other1 = near1
    (mid1,) = call_add(mid_kernel, "mid", [pltpu.VMEM((2, PIXELS, width), jnp.float32)], keep1, across1)
    previous, own = call_add(split_kernel, "split", [bf16, f32], mid1, other1)
    previous = lax.ppermute(previous, "tp", hop(1))
    result = added(own, opposite, following, previous).astype(jnp.bfloat16)
    bands = lax.all_to_all(result.reshape(BANDS, LOW, width), "row", 0, 0)
    return bands.reshape(2, 8, LOW, width).transpose(1, 0, 2, 3).reshape(1, 8, 8, width)


def solution(mesh):
    placed = (
        P(None, "row", None, "tp"),
        P(None, "tp", None, None),
        P(None, "tp"),
        P(None, "tp", None),
    )
    return jax.shard_map(
        on_device, mesh=mesh, in_specs=placed, out_specs=P(None, "row", "tp", None), check_vma=False
    )
```

```python
import functools

import jax
import jax.numpy as jnp
from jax import lax
from jax.experimental import pallas as pl
from jax.experimental.pallas import tpu as pltpu
from jax.sharding import PartitionSpec as P


DISTANCES = (1, 2, 4)
BANDS = 16
SPOTS = 16
LOW = 4
PIXELS = BANDS * LOW
PAD = 4
TAPS = 9
GROUP = 64
VMEM_SPEC = pl.BlockSpec(memory_space=pltpu.VMEM)


def in_vmem(array):
    return pltpu.with_memory_space_constraint(array, pltpu.VMEM)


def swap_halves(even, odd):
    low = lax.broadcasted_iota(jnp.int32, even.shape, even.ndim - 2) < LOW
    axis = even.ndim - 2
    first = jnp.where(low, even, pltpu.roll(odd, LOW, axis))
    second = jnp.where(low, pltpu.roll(even, LOW, axis), odd)
    return first, second


def pack_kernel(x_ref, out_ref):
    chan = x_ref.shape[2]
    for j in range(8):
        v = x_ref[j].astype(jnp.float32).reshape(8, 2, 8, chan)
        first, second = swap_halves(v[:, 0], v[:, 1])
        out_ref[j] = first.reshape(PIXELS, chan).astype(jnp.bfloat16)
        out_ref[8 + j] = second.reshape(PIXELS, chan).astype(jnp.bfloat16)


def pack(x):
    return pl.pallas_call(
        pack_kernel,
        out_specs=VMEM_SPEC,
        out_shape=pltpu.VMEM((16, PIXELS, x.shape[2]), jnp.bfloat16),
        compiler_params=pltpu.CompilerParams(vmem_limit_bytes=60 * 2**20),
        name="pack",
    )(x)


def turn_kernel(w_ref, out_ref):
    for tap in range(TAPS):
        start, width = (tap // 2) * 128, 128 if tap < 8 else 64
        place = lax.broadcasted_iota(jnp.int32, (GROUP, width), 0) + (tap % 2) * GROUP
        pick = (place == lax.broadcasted_iota(jnp.int32, (GROUP, width), 1)).astype(jnp.float32).astype(jnp.bfloat16)
        for arm in range(3):
            slab = w_ref[arm, :, start : start + width]
            turned = lax.dot_general(pick, slab, (((1,), (1,)), ((), ())), preferred_element_type=jnp.float32)
            out_ref[arm, tap * GROUP : (tap + 1) * GROUP, :] = turned.astype(jnp.bfloat16)


def turn(conv_weight):
    chan = conv_weight.shape[1] * conv_weight.shape[2]
    return pl.pallas_call(
        turn_kernel,
        in_specs=[VMEM_SPEC],
        out_specs=VMEM_SPEC,
        out_shape=pltpu.VMEM((3, TAPS * GROUP, chan), jnp.bfloat16),
        compiler_params=pltpu.CompilerParams(vmem_limit_bytes=16 * 2**20),
        name="turn",
    )(conv_weight.reshape(3, chan, -1))


def shifted(v, by):
    chan = v.shape[1]
    row = lax.broadcasted_iota(jnp.int32, v.shape, 0)
    if by == 0:
        return v
    if by == LOW:
        return jnp.where(row >= LOW, pltpu.roll(v, LOW, 0), 0.0)
    if by == -LOW:
        return jnp.where(row < PIXELS - LOW, pltpu.roll(v, PIXELS - LOW, 0), 0.0)
    zeros = jnp.zeros((abs(by), chan), v.dtype)
    if by > 0:
        return jnp.concatenate([zeros, v[: PIXELS - by]], axis=0)
    return jnp.concatenate([v[-by:], zeros], axis=0)


SHIFTS = (0, 1, -1, 2, -2, 4, -4)


def spread_kernel(x_ref, s_ref):
    chan = x_ref.shape[2]
    zeros = jnp.zeros((len(SHIFTS), PAD, PIXELS, chan), jnp.bfloat16)
    s_ref[:, :PAD] = zeros
    s_ref[:, PAD + SPOTS :] = zeros
    for quad in range(4):
        v = x_ref[:, quad * 16 : (quad + 1) * 16, :].astype(jnp.float32).reshape(8, 2, 2, 8, chan)
        halves = swap_halves(v[:, 0], v[:, 1])
        for pair in range(2):
            for side in range(2):
                spot = PAD + 4 * quad + 2 * pair + side
                mine = halves[side][:, pair].reshape(PIXELS, chan)
                for at, shift in enumerate(SHIFTS):
                    s_ref[at, spot] = shifted(mine, LOW * shift).astype(jnp.bfloat16)


def spread(x):
    return pl.pallas_call(
        spread_kernel,
        in_specs=[VMEM_SPEC],
        out_specs=VMEM_SPEC,
        out_shape=pltpu.VMEM((len(SHIFTS), SPOTS + 2 * PAD, PIXELS, x.shape[2]), jnp.bfloat16),
        compiler_params=pltpu.CompilerParams(vmem_limit_bytes=16 * 2**20),
        name="spread",
    )(x)


def added(*terms):
    return sum(term.astype(jnp.float32) for term in terms)


def far_kernel(keep_ref, other_ref, out_ref):
    for at in range(2):
        out_ref[at] = added(keep_ref[at], other_ref[at]).astype(jnp.bfloat16)


def mid_kernel(keep_ref, across_ref, out_ref):
    for at in range(2):
        out_ref[at] = added(keep_ref[at], across_ref[at])


def split_kernel(mid_ref, other_ref, first_ref, second_ref):
    for at, out_ref in enumerate((first_ref, second_ref)):
        out_ref[...] = added(mid_ref[at], other_ref[at]).astype(out_ref.dtype)


def near_kernel(keep_ref, other_ref, across_ref, first_ref, second_ref):
    for at, out_ref in enumerate((first_ref, second_ref)):
        out_ref[...] = added(keep_ref[at], other_ref[at], across_ref[at]).astype(out_ref.dtype)


def call_add(kernel, name, out, *terms):
    return pl.pallas_call(
        kernel,
        in_specs=[VMEM_SPEC] * len(terms),
        out_specs=[VMEM_SPEC] * len(out),
        out_shape=out,
        compiler_params=pltpu.CompilerParams(vmem_limit_bytes=8 * 2**20),
        name=name,
    )(*[in_vmem(term) for term in terms])


def head_kernel(chunk, spot_ref, s_ref, w_ref, bias_ref, unite_ref, *refs):
    send_ref, keep_ref = refs[-2:]
    chan = s_ref.shape[3]
    spots = [PAD + spot_ref[chunk, at] for at in range(4)]
    groups = chan // GROUP
    column = lax.broadcasted_iota(jnp.int32, (GROUP, chan), 1) // GROUP
    masks = [(column == group).astype(jnp.float32).astype(jnp.bfloat16) for group in range(groups)]
    hidden = []
    for arm, distance in enumerate(DISTANCES):
        total = None
        for kh in range(3):
            at = SHIFTS.index((1 - kh) * distance)
            for kw in range(3):
                left = jnp.concatenate([s_ref[at, spot + (kw - 1) * distance] for spot in spots], axis=0)
                tap = 3 * kh + kw
                narrow = w_ref[arm, tap * GROUP : (tap + 1) * GROUP, :]
                wide = jnp.concatenate([narrow * mask for mask in masks], axis=0)
                part = jnp.dot(left, wide, preferred_element_type=jnp.float32)
                total = part if total is None else total + part
        summed = total + bias_ref[arm : arm + 1, :]
        hidden.append((0.5 * summed * (1.0 + lax.erf(summed * (0.5**0.5)))).astype(jnp.bfloat16))
    term = None
    for arm in range(3):
        part = jnp.dot(hidden[arm], unite_ref[arm], preferred_element_type=jnp.float32)
        term = part if term is None else term + part
    term = term.reshape(4, PIXELS, -1)
    send_ref[...] = term[:2].astype(jnp.bfloat16)
    keep_ref[...] = term[2:]


def head_terms(chunk, spots, spread_x, wide, bias, unite, after):
    out = [pltpu.VMEM((2, PIXELS, unite.shape[2]), dtype) for dtype in (jnp.bfloat16, jnp.float32)]
    return pl.pallas_call(
        functools.partial(head_kernel, chunk),
        in_specs=[pl.BlockSpec(memory_space=pltpu.SMEM)] + [VMEM_SPEC] * 4 + [pl.BlockSpec(memory_space=pl.ANY)] * len(after),
        out_specs=[VMEM_SPEC] * 2,
        out_shape=out,
        compiler_params=pltpu.CompilerParams(vmem_limit_bytes=16 * 2**20),
        name="head",
    )(spots, spread_x, wide, bias, unite, *after)


def finish_kernel(x_ref, out_ref):
    for j in range(8):
        halves = [x_ref[8 * side + j].astype(jnp.float32) for side in range(2)]
        out_ref[j] = jnp.concatenate(halves, axis=0).astype(jnp.bfloat16)


def finish(bands):
    return pl.pallas_call(
        finish_kernel,
        in_specs=[VMEM_SPEC],
        out_specs=VMEM_SPEC,
        out_shape=jax.ShapeDtypeStruct((8, 2 * LOW, bands.shape[2]), jnp.bfloat16),
        compiler_params=pltpu.CompilerParams(vmem_limit_bytes=16 * 2**20),
        name="finish",
    )(bands)


CHUNKS = (((2, 1), (3, 1)), ((1, 1), (0, 1)), ((2, 0), (3, 0)), ((1, 0), (0, 0)))
SWAP = [(i, i ^ 1) for i in range(16)]
FAR = [(i, i ^ 2) for i in range(16)]


def hop(ahead):
    return [(i, (i + 4 * ahead) % 16) for i in range(16)]


def on_device(feature_map, conv_weight, branch_bias, unite_weight):
    at = lax.axis_index("tp").astype(jnp.int32)
    chip_x, chip_y, core = at // 4, (at // 2) % 2, at % 2
    spots = jnp.stack([
        jnp.stack([4 * ((chip_x + ahead) % 4) + 2 * ((chip_y + across) % 2) + (core + side) % 2 for side in (1, 0) for ahead, across in chunk])
        for chunk in CHUNKS
    ])
    packed = pack(feature_map[0])
    wide = in_vmem(turn(conv_weight))
    mine = lax.all_to_all(packed, "row", 0, 0)
    spread_x = spread(mine)
    unite, bias = in_vmem(unite_weight), in_vmem(branch_bias)
    width = unite_weight.shape[2]
    bf16, f32 = (pltpu.VMEM((PIXELS, width), dtype) for dtype in (jnp.bfloat16, jnp.float32))
    both = pltpu.VMEM((2, PIXELS, width), jnp.bfloat16)

    def head(chunk, *after):
        send, keep = head_terms(chunk, spots, spread_x, wide, bias, unite, after)
        return keep, lax.ppermute(send, "tp", SWAP)

    far0, far1 = head(0), head(1)
    (far0,) = call_add(far_kernel, "far", [both], *far0)
    across0 = lax.ppermute(far0, "tp", FAR)
    near0 = head(2, far0)
    (far1,) = call_add(far_kernel, "far", [both], *far1)
    across1 = lax.ppermute(far1, "tp", FAR)
    near1 = head(3, far1)
    opposite, following = call_add(near_kernel, "near", [bf16, bf16], *near0, across0)
    opposite, following = lax.ppermute(opposite, "tp", hop(2)), lax.ppermute(following, "tp", hop(3))
    keep1, other1 = near1
    (mid1,) = call_add(mid_kernel, "mid", [pltpu.VMEM((2, PIXELS, width), jnp.float32)], keep1, across1)
    previous, own = call_add(split_kernel, "split", [bf16, f32], mid1, other1)
    previous = lax.ppermute(previous, "tp", hop(1))
    result = added(own, opposite, following, previous).astype(jnp.bfloat16)
    bands = lax.all_to_all(result.reshape(BANDS, LOW, width), "row", 0, 0)
    return finish(bands)[None]


def solution(mesh):
    placed = (
        P(None, "row", None, "tp"),
        P(None, "tp", None, None),
        P(None, "tp"),
        P(None, "tp", None),
    )
    return jax.shard_map(
        on_device, mesh=mesh, in_specs=placed, out_specs=P(None, "row", "tp", None), check_vma=False
    )
```

```python
import functools

import jax
import jax.numpy as jnp
from jax import lax
from jax.experimental import pallas as pl
from jax.experimental.pallas import tpu as pltpu
from jax.sharding import PartitionSpec as P


DISTANCES = (1, 2, 4)
BANDS = 16
SPOTS = 16
LOW = 4
PIXELS = BANDS * LOW
PAD = 4
TAPS = 9
GROUP = 64
VMEM_SPEC = pl.BlockSpec(memory_space=pltpu.VMEM)


def in_vmem(array):
    return pltpu.with_memory_space_constraint(array, pltpu.VMEM)


def swap_halves(even, odd):
    low = lax.broadcasted_iota(jnp.int32, even.shape, even.ndim - 2) < LOW
    axis = even.ndim - 2
    first = jnp.where(low, even, pltpu.roll(odd, LOW, axis))
    second = jnp.where(low, pltpu.roll(even, LOW, axis), odd)
    return first, second


def pack_kernel(x_ref, out_ref):
    chan = x_ref.shape[2]
    for j in range(8):
        v = x_ref[j].astype(jnp.float32).reshape(8, 2, 8, chan)
        first, second = swap_halves(v[:, 0], v[:, 1])
        out_ref[j] = first.reshape(PIXELS, chan).astype(jnp.bfloat16)
        out_ref[8 + j] = second.reshape(PIXELS, chan).astype(jnp.bfloat16)


def pack(x):
    return pl.pallas_call(
        pack_kernel,
        out_specs=VMEM_SPEC,
        out_shape=pltpu.VMEM((16, PIXELS, x.shape[2]), jnp.bfloat16),
        compiler_params=pltpu.CompilerParams(vmem_limit_bytes=16 * 2**20),
        name="pack",
    )(x)


def turn_kernel(w_ref, out_ref):
    for tap in range(TAPS):
        start, width = (tap // 2) * 128, 128 if tap < 8 else 64
        place = lax.broadcasted_iota(jnp.int32, (GROUP, width), 0) + (tap % 2) * GROUP
        pick = (place == lax.broadcasted_iota(jnp.int32, (GROUP, width), 1)).astype(jnp.float32).astype(jnp.bfloat16)
        for arm in range(3):
            slab = w_ref[arm, :, start : start + width]
            turned = lax.dot_general(pick, slab, (((1,), (1,)), ((), ())), preferred_element_type=jnp.float32)
            out_ref[arm, tap * GROUP : (tap + 1) * GROUP, :] = turned.astype(jnp.bfloat16)


def turn(conv_weight):
    chan = conv_weight.shape[1] * conv_weight.shape[2]
    return pl.pallas_call(
        turn_kernel,
        in_specs=[VMEM_SPEC],
        out_specs=VMEM_SPEC,
        out_shape=pltpu.VMEM((3, TAPS * GROUP, chan), jnp.bfloat16),
        compiler_params=pltpu.CompilerParams(vmem_limit_bytes=16 * 2**20),
        name="turn",
    )(conv_weight.reshape(3, chan, -1))


def shifted(v, by):
    chan = v.shape[1]
    row = lax.broadcasted_iota(jnp.int32, v.shape, 0)
    if by == 0:
        return v
    if by == LOW:
        return jnp.where(row >= LOW, pltpu.roll(v, LOW, 0), 0.0)
    if by == -LOW:
        return jnp.where(row < PIXELS - LOW, pltpu.roll(v, PIXELS - LOW, 0), 0.0)
    zeros = jnp.zeros((abs(by), chan), v.dtype)
    if by > 0:
        return jnp.concatenate([zeros, v[: PIXELS - by]], axis=0)
    return jnp.concatenate([v[-by:], zeros], axis=0)


SHIFTS = (0, 1, -1, 2, -2, 4, -4)


def spread_kernel(x_ref, s_ref):
    chan = x_ref.shape[2]
    zeros = jnp.zeros((len(SHIFTS), PAD, PIXELS, chan), jnp.bfloat16)
    s_ref[:, :PAD] = zeros
    s_ref[:, PAD + SPOTS :] = zeros
    for quad in range(4):
        v = x_ref[:, quad * 16 : (quad + 1) * 16, :].astype(jnp.float32).reshape(8, 2, 2, 8, chan)
        halves = swap_halves(v[:, 0], v[:, 1])
        for pair in range(2):
            for side in range(2):
                spot = PAD + 4 * quad + 2 * pair + side
                mine = halves[side][:, pair].reshape(PIXELS, chan)
                for at, shift in enumerate(SHIFTS):
                    s_ref[at, spot] = shifted(mine, LOW * shift).astype(jnp.bfloat16)


def spread(x):
    return pl.pallas_call(
        spread_kernel,
        in_specs=[VMEM_SPEC],
        out_specs=VMEM_SPEC,
        out_shape=pltpu.VMEM((len(SHIFTS), SPOTS + 2 * PAD, PIXELS, x.shape[2]), jnp.bfloat16),
        compiler_params=pltpu.CompilerParams(vmem_limit_bytes=16 * 2**20),
        name="spread",
    )(x)


def added(*terms):
    return sum(term.astype(jnp.float32) for term in terms)


def far_kernel(keep_ref, other_ref, out_ref):
    for at in range(2):
        out_ref[at] = added(keep_ref[at], other_ref[at]).astype(jnp.bfloat16)


def mid_kernel(keep_ref, across_ref, out_ref):
    for at in range(2):
        out_ref[at] = added(keep_ref[at], across_ref[at])


def split_kernel(mid_ref, other_ref, first_ref, second_ref):
    for at, out_ref in enumerate((first_ref, second_ref)):
        out_ref[...] = added(mid_ref[at], other_ref[at]).astype(out_ref.dtype)


def near_kernel(keep_ref, other_ref, across_ref, first_ref, second_ref):
    for at, out_ref in enumerate((first_ref, second_ref)):
        out_ref[...] = added(keep_ref[at], other_ref[at], across_ref[at]).astype(out_ref.dtype)


def call_add(kernel, name, out, *terms):
    return pl.pallas_call(
        kernel,
        in_specs=[VMEM_SPEC] * len(terms),
        out_specs=[VMEM_SPEC] * len(out),
        out_shape=out,
        compiler_params=pltpu.CompilerParams(vmem_limit_bytes=8 * 2**20),
        name=name,
    )(*[in_vmem(term) for term in terms])


def head_kernel(chunk, spot_ref, s_ref, w_ref, bias_ref, unite_ref, *refs):
    send_ref, keep_ref = refs[-2:]
    chan = s_ref.shape[3]
    spots = [PAD + spot_ref[chunk, at] for at in range(4)]
    groups = chan // GROUP
    column = lax.broadcasted_iota(jnp.int32, (GROUP, chan), 1) // GROUP
    masks = [(column == group).astype(jnp.float32).astype(jnp.bfloat16) for group in range(groups)]
    hidden = []
    for arm, distance in enumerate(DISTANCES):
        total = None
        for kh in range(3):
            at = SHIFTS.index((1 - kh) * distance)
            for kw in range(3):
                left = jnp.concatenate([s_ref[at, spot + (kw - 1) * distance] for spot in spots], axis=0)
                tap = 3 * kh + kw
                narrow = w_ref[arm, tap * GROUP : (tap + 1) * GROUP, :]
                wide = jnp.concatenate([narrow * mask for mask in masks], axis=0)
                part = jnp.dot(left, wide, preferred_element_type=jnp.float32)
                total = part if total is None else total + part
        summed = total + bias_ref[arm : arm + 1, :]
        hidden.append((0.5 * summed * (1.0 + lax.erf(summed * (0.5**0.5)))).astype(jnp.bfloat16))
    term = None
    for arm in range(3):
        part = jnp.dot(hidden[arm], unite_ref[arm], preferred_element_type=jnp.float32)
        term = part if term is None else term + part
    term = term.reshape(4, PIXELS, -1)
    send_ref[...] = term[:2].astype(jnp.bfloat16)
    keep_ref[...] = term[2:]


def head_terms(chunk, spots, spread_x, wide, bias, unite, after):
    out = [pltpu.VMEM((2, PIXELS, unite.shape[2]), dtype) for dtype in (jnp.bfloat16, jnp.float32)]
    return pl.pallas_call(
        functools.partial(head_kernel, chunk),
        in_specs=[pl.BlockSpec(memory_space=pltpu.SMEM)] + [VMEM_SPEC] * 4 + [pl.BlockSpec(memory_space=pl.ANY)] * len(after),
        out_specs=[VMEM_SPEC] * 2,
        out_shape=out,
        compiler_params=pltpu.CompilerParams(vmem_limit_bytes=16 * 2**20),
        name="head",
    )(spots, spread_x, wide, bias, unite, *after)


CHUNKS = (((2, 1), (3, 1)), ((1, 1), (0, 1)), ((2, 0), (3, 0)), ((1, 0), (0, 0)))
SWAP = [(i, i ^ 1) for i in range(16)]
FAR = [(i, i ^ 2) for i in range(16)]


def hop(ahead):
    return [(i, (i + 4 * ahead) % 16) for i in range(16)]


def on_device(feature_map, conv_weight, branch_bias, unite_weight):
    at = lax.axis_index("tp").astype(jnp.int32)
    chip_x, chip_y, core = at // 4, (at // 2) % 2, at % 2
    spots = jnp.stack([
        jnp.stack([4 * ((chip_x + ahead) % 4) + 2 * ((chip_y + across) % 2) + (core + side) % 2 for side in (1, 0) for ahead, across in chunk])
        for chunk in CHUNKS
    ])
    packed, unite_weight = lax.optimization_barrier((pack(feature_map[0]), unite_weight))
    wide = in_vmem(turn(conv_weight))
    mine = lax.all_to_all(packed, "row", 0, 0)
    spread_x = spread(mine)
    unite, bias = in_vmem(unite_weight), in_vmem(branch_bias)
    width = unite_weight.shape[2]
    bf16, f32 = (pltpu.VMEM((PIXELS, width), dtype) for dtype in (jnp.bfloat16, jnp.float32))
    both = pltpu.VMEM((2, PIXELS, width), jnp.bfloat16)

    def head(chunk, *after):
        send, keep = head_terms(chunk, spots, spread_x, wide, bias, unite, after)
        return keep, lax.ppermute(send, "tp", SWAP)

    far0, far1 = head(0), head(1)
    (far0,) = call_add(far_kernel, "far", [both], *far0)
    across0 = lax.ppermute(far0, "tp", FAR)
    near0 = head(2, far0)
    (far1,) = call_add(far_kernel, "far", [both], *far1)
    across1 = lax.ppermute(far1, "tp", FAR)
    near1 = head(3, far1)
    opposite, following = call_add(near_kernel, "near", [bf16, bf16], *near0, across0)
    opposite, following = lax.ppermute(opposite, "tp", hop(2)), lax.ppermute(following, "tp", hop(3))
    keep1, other1 = near1
    (mid1,) = call_add(mid_kernel, "mid", [pltpu.VMEM((2, PIXELS, width), jnp.float32)], keep1, across1)
    previous, own = call_add(split_kernel, "split", [bf16, f32], mid1, other1)
    previous = lax.ppermute(previous, "tp", hop(1))
    result = added(own, opposite, following, previous).astype(jnp.bfloat16)
    bands = lax.all_to_all(result.reshape(BANDS, LOW, width), "row", 0, 0)
    return bands.reshape(2, 8, LOW, width).transpose(1, 0, 2, 3).reshape(1, 8, 8, width)


def solution(mesh):
    placed = (
        P(None, "row", None, "tp"),
        P(None, "tp", None, None),
        P(None, "tp"),
        P(None, "tp", None),
    )
    return jax.shard_map(
        on_device, mesh=mesh, in_specs=placed, out_specs=P(None, "row", "tp", None), check_vma=False
    )
```
